32 devices in a mesh: seq: 8 (over z, y), heads: 4 (over x, core).
Axes of the slice: x: 2, y: 2, z: 4, core: 2. Of those that a mesh axis runs over, the one named last changes fastest.
Arguments:
- fwd_tokens: bfloat16 [2048, 4096], P('seq'), may hold values from -6 to 6
- bwd_tokens: bfloat16 [2048, 4096], P('seq'), may hold values from -6 to 6
- qkv_weight: bfloat16 [4096, 3072], P('seq', 'heads'), may hold values from -0.09375 to 0.09375
- head_gain: float32 [1024], P('heads'), may hold values from 0.1 to 1.9
- out_cotangent: float32 [2048, 1024], P('seq', 'heads'), may hold values from -6 to 6
- initial_state: float32 [2, 4, 256, 256], P(None, 'heads'), may hold values from -192 to 192
Outputs:
- fwd_output: float32 [2048, 1024], P('seq', 'heads')
- bwd_token_grad: bfloat16 [2048, 4096], P('seq', 'heads')
The draws below stay inside these ranges and needn't reach their ends.
All inputs are finite; a program needn't handle non-finite values.
Results may differ from the reference program's by a relative error of at most 0.02.
Values may be sent and summed in bfloat16 or wider, within the bound.
A program may use at most 64 MiB of HBM per device.

```python
import jax
import jax.numpy as jnp
from jax import lax

D = 4096
DH = 256
TOK_DEV = 256
HEADS = 4
TOKENS = 2048


def shard_levels(own_key, dims, shards, low, top_value):
    loudness, own = 1.0, jax.random.fold_in(own_key, 6)
    for position, shards_of in shards:
        steps = jnp.exp(jax.random.uniform(jax.random.fold_in(own, position), (shards_of,), jnp.float32, low / len(shards), top_value / len(shards)))
        loudness = loudness * jnp.repeat(steps, dims[position] // shards_of).reshape([-1 if axis == position else 1 for axis in range(len(dims))])
    return loudness


def bell_draw(own_key, extent, width, most, shards=(), dtype=jnp.bfloat16):
    array = jax.random.normal(own_key, extent, jnp.float32) * width
    if len(shards) > 0:
        array = shard_levels(own_key, extent, shards, -0.22, 0.18) * array
    return jnp.clip(array, min=-most, max=most).astype(dtype)


def setup_inputs(seed: int = 0) -> dict:
    key_list = jax.random.split(jax.random.key(seed), 7)
    fwd_tokens = bell_draw(key_list[0], (TOKENS, D), 1.0, 6.0, ((0, 8),))
    bwd_tokens = bell_draw(key_list[1], (TOKENS, D), 1.0, 6.0, ((0, 8),))
    qkv_weight = bell_draw(key_list[2], (D, HEADS * 3 * DH), D ** -0.5, 0.09375, ((0, 8), (1, 4)))
    head_gain = jnp.clip(1.0 + 0.18 * jax.random.normal(key_list[3], (HEADS * DH,), jnp.float32), 0.1, 1.9)
    out_cotangent = bell_draw(key_list[4], (TOKENS, HEADS * DH), 1.0, 6.0, ((0, 8), (1, 4)), jnp.float32)
    initial_state = bell_draw(key_list[5], (2, HEADS, DH, DH), (DH // 8), 192.0, ((1, 4),), jnp.float32)
    return {"fwd_tokens": fwd_tokens, "bwd_tokens": bwd_tokens, "qkv_weight": qkv_weight, "head_gain": head_gain, "out_cotangent": out_cotangent, "initial_state": initial_state}


highest = lax.Precision.HIGHEST
epsilon = 1e-06

def span_forward(queries, keys, values, causal, carried):
    states = jnp.einsum('cti,ctj->cij', keys, values, precision=highest)
    prefix = jnp.cumsum(states, 0) - states + carried
    scores = jnp.einsum('cti,csi->cts', queries, keys, precision=highest) * causal
    output = jnp.einsum('cti,cij->ctj', queries, prefix, precision=highest) + jnp.einsum('cts,csj->ctj', scores, values, precision=highest)
    return (output, prefix, scores)

def head_pass(fwd_tokens, bwd_tokens, weight_head, gain_head, grad_head, carried):
    spans = TOKENS // TOK_DEV
    causal = jnp.tril(jnp.ones((TOK_DEV, TOK_DEV), jnp.float32))
    proj_fwd = jnp.dot(fwd_tokens, weight_head, preferred_element_type=jnp.float32).reshape(spans, TOK_DEV, 3 * DH)
    proj_bwd = jnp.dot(bwd_tokens, weight_head, preferred_element_type=jnp.float32).reshape(spans, TOK_DEV, 3 * DH)
    out_fwd, prefix_unused, scores_unused = span_forward(proj_fwd[..., :DH], proj_fwd[..., DH:2 * DH], proj_fwd[..., 2 * DH:], causal, carried[0])
    scale_fwd = lax.rsqrt(lax.optimization_barrier(jnp.mean(out_fwd * out_fwd, -1, keepdims=True)) + epsilon)
    normed = (out_fwd * scale_fwd * gain_head).reshape(TOKENS, DH)
    queries = proj_bwd[..., :DH]
    keys = proj_bwd[..., DH:2 * DH]
    values = proj_bwd[..., 2 * DH:]
    output, prefix, scores = span_forward(queries, keys, values, causal, carried[1])
    scale = lax.rsqrt(lax.optimization_barrier(jnp.mean(output * output, -1, keepdims=True)) + epsilon)
    weighted = grad_head.reshape(spans, TOK_DEV, DH) * gain_head
    d_out = scale * weighted - output * scale ** 3 * lax.optimization_barrier(jnp.mean(output * weighted, -1, keepdims=True))
    d_states = jnp.einsum('cti,ctj->cij', queries, d_out, precision=highest)
    suffix = jnp.cumsum(d_states[::-1], 0)[::-1] - d_states
    d_scores = jnp.einsum('ctj,csj->cts', d_out, values, precision=highest) * causal
    d_query = jnp.einsum('ctj,cij->cti', d_out, prefix, precision=highest) + jnp.einsum('cts,csi->cti', d_scores, keys, precision=highest)
    d_key = jnp.einsum('csj,cij->csi', values, suffix, precision=highest) + jnp.einsum('cts,cti->csi', d_scores, queries, precision=highest)
    d_value = jnp.einsum('csi,cij->csj', keys, suffix, precision=highest) + jnp.einsum('cts,ctj->csj', scores, d_out, precision=highest)
    d_proj = jnp.concatenate([d_query, d_key, d_value], -1).reshape(TOKENS, 3 * DH).astype(jnp.bfloat16)
    partial_value = jnp.dot(d_proj, weight_head.T, preferred_element_type=jnp.float32).astype(jnp.bfloat16)
    return (normed, partial_value)

def reference(fwd_tokens, bwd_tokens, qkv_weight, head_gain, out_cotangent, initial_state):
    weights = qkv_weight.reshape(D, HEADS, 3 * DH).transpose(1, 0, 2)
    gains = head_gain.reshape(HEADS, DH)
    grads = out_cotangent.reshape(TOKENS, HEADS, DH).transpose(1, 0, 2)
    carried = initial_state.transpose(1, 0, 2, 3)

    def step(total, items):
        normed, partial_value = head_pass(fwd_tokens, bwd_tokens, items[0], items[1], items[2], items[3])
        partial_value = lax.optimization_barrier(partial_value)
        return (total + partial_value.astype(jnp.float32), normed)
    total, normed = lax.scan(step, jnp.zeros((TOKENS, D), jnp.float32), (weights, gains, grads, carried))
    fwd_output = normed.transpose(1, 0, 2).reshape(TOKENS, HEADS * DH)
    return (fwd_output, total.astype(jnp.bfloat16))
```

```python
import functools

import jax
import jax.numpy as jnp
from jax import lax
from jax.experimental import pallas as pl
from jax.experimental.pallas import tpu as pltpu
from jax.sharding import PartitionSpec as P

MESH = pl.DeviceIdType.MESH
BF16 = jnp.bfloat16
F32 = jnp.float32
epsilon = 1e-06


def dot(a, b):
    return lax.dot_general(a, b, (((1,), (0,)), ((), ())), preferred_element_type=F32)


def dot_t(a, b):
    return lax.dot_general(a, b, (((1,), (1,)), ((), ())), preferred_element_type=F32)


def t_dot(a, b):
    return lax.dot_general(a, b, (((0,), (0,)), ((), ())), preferred_element_type=F32)


def kernel(
    n,
    hn,
    xf_ref,
    xb_ref,
    w_ref,
    gain_ref,
    cot_ref,
    init_ref,
    of_ref,
    ob_ref,
    xbuf,
    wbuf,
    acc,
    cot,
    init,
    st_own,
    st_peer,
    st_tot,
    st_z,
    st_half,
    st_far,
    half32,
    whole32,
    c_send,
    c_recv,
    x_send,
    x_recv,
    load_sem,
    wsend,
    wrecv,
    st_ssem,
    st_rsem,
    z_ssem,
    z_rsem,
    c_ssem,
    c_rsem,
    x_ssem,
    x_rsem,
):
    s, h = lax.axis_index("seq"), lax.axis_index("heads")
    chain, pairs = n // 2, hn // 2
    a, b = lax.div(s, 2), lax.rem(s, 2)
    xh, c = lax.div(h, 2), lax.rem(h, 2)
    mate = a * 2 + 1 - b
    twin = xh * 2 + 1 - c
    tokens = xf_ref.shape[0]
    depth = w_ref.shape[0]
    width = gain_ref.shape[1]
    half = width // 2
    feat = ob_ref.shape[1]

    def rows_of(source):
        return pl.ds(pl.multiple_of(source * depth, depth), depth)

    w_loads = [
        pltpu.make_async_copy(
            w_ref.at[:, pl.ds(p * width, width)], wbuf.at[p, rows_of(s)], load_sem.at[p]
        )
        for p in range(3)
    ]
    x_loads = [
        pltpu.make_async_copy(xf_ref, xbuf.at[pl.ds(0, tokens)], load_sem.at[3]),
        pltpu.make_async_copy(xb_ref, xbuf.at[pl.ds(tokens, tokens)], load_sem.at[4]),
    ]
    o_loads = [
        pltpu.make_async_copy(cot_ref, cot, load_sem.at[5]),
        pltpu.make_async_copy(init_ref, init, load_sem.at[6]),
    ]
    for p in (1, 2, 0):
        w_loads[p].start()
    for load in x_loads + o_loads:
        load.start()

    barrier = pltpu.get_barrier_semaphore()

    def greet(seq_index, head_index):
        pl.semaphore_signal(barrier, inc=1, device_id=(seq_index, head_index), device_id_type=MESH)

    for e in range(1, chain):
        greet(lax.rem(a + e, chain) * 2 + b, h)
    greet(mate, h)
    for e in range(1, pairs):
        greet(s, lax.rem(xh + e, pairs) * 2 + c)
    greet(s, twin)
    pl.semaphore_wait(barrier, chain + pairs)

    UP, DOWN, CROSS = 0, 1, 2

    def shard_copy(p, sa, sb, way):
        source = sa * 2 + sb
        to = {UP: s + 2, DOWN: s - 2, CROSS: mate}[way]
        return pltpu.make_async_remote_copy(
            src_ref=wbuf.at[p, rows_of(source)],
            dst_ref=wbuf.at[p, rows_of(source)],
            send_sem=wsend.at[way, sa, p],
            recv_sem=wrecv.at[source, p],
            device_id=(to, h),
            device_id_type=MESH,
        )

    def project(source, pieces):
        x = xbuf[:, pl.ds(pl.multiple_of(source * depth, depth), depth)]
        for p in pieces:
            acc[p] += dot(x, wbuf[p, rows_of(source)])

    def start_up(p, sa):
        @pl.when(a < chain - 1)
        def _():
            shard_copy(p, sa, b, UP).start()

    def start_down(p, sa):
        @pl.when(a > 0)
        def _():
            shard_copy(p, sa, b, DOWN).start()

    def arrivals(d, pieces, then_own):
        @pl.when(a - d >= 0)
        def _():
            for p in pieces:
                shard_copy(p, a - d, b, CROSS).wait_recv()
                start_up(p, a - d)
                shard_copy(p, a - d, b, CROSS).start()

            @pl.when(a - d == 0)
            def _():
                for p in then_own:
                    start_up(p, a)

        @pl.when(a + d < chain)
        def _():
            for p in pieces:
                shard_copy(p, a + d, b, CROSS).wait_recv()
                start_down(p, a + d)
                shard_copy(p, a + d, b, CROSS).start()

            @pl.when(a + d == chain - 1)
            def _():
                for p in then_own:
                    start_down(p, a)

        @pl.when(a - d >= 0)
        def _():
            project((a - d) * 2 + b, pieces)

        @pl.when(a + d < chain)
        def _():
            project((a + d) * 2 + b, pieces)

    def crossed(sa, pieces):
        for p in pieces:
            shard_copy(p, sa, 1 - b, CROSS).wait_recv()
        project(sa * 2 + 1 - b, pieces)

    def crossings(d, pieces):
        @pl.when(a - d >= 0)
        def _():
            crossed(a - d, pieces)

        @pl.when((a + d < chain) & (d > 0))
        def _():
            crossed(a + d, pieces)

    kv, q_only = (1, 2), (0,)
    for p in kv:
        w_loads[p].wait()
        start_up(p, a)
        start_down(p, a)
        shard_copy(p, a, b, CROSS).start()
    w_loads[0].wait()

    @pl.when(a == 0)
    def _():
        start_up(0, a)

    @pl.when(a == chain - 1)
    def _():
        start_down(0, a)

    acc[...] = jnp.zeros_like(acc)
    for load in x_loads:
        load.wait()
    project(s, (0, 1, 2))

    def kv_lap(d, carry):
        arrivals(d, kv, q_only)
        crossings(d - 1, kv)
        return carry

    lax.fori_loop(1, chain, kv_lap, 0)
    shard_copy(0, a, b, CROSS).start()
    crossings(chain - 1, kv)

    my_half = pl.ds(pl.multiple_of(b * half, half), half)
    far_half = pl.ds(pl.multiple_of((1 - b) * half, half), half)

    def step1_copy(i):
        return pltpu.make_async_remote_copy(
            src_ref=st_own.at[i],
            dst_ref=st_peer.at[i],
            send_sem=st_ssem.at[i, 0],
            recv_sem=st_rsem.at[i, 0],
            device_id=(mate, h),
            device_id_type=MESH,
        )

    def step2_copy(i, to, slot):
        return pltpu.make_async_remote_copy(
            src_ref=st_tot.at[i],
            dst_ref=st_z.at[i, slot],
            send_sem=z_ssem.at[i, to],
            recv_sem=z_rsem.at[i, slot],
            device_id=(to * 2 + b, h),
            device_id_type=MESH,
        )

    def step3_copy(i):
        return pltpu.make_async_remote_copy(
            src_ref=st_half.at[i],
            dst_ref=st_far.at[i],
            send_sem=st_ssem.at[i, 1],
            recv_sem=st_rsem.at[i, 1],
            device_id=(mate, h),
            device_id_type=MESH,
        )

    def after(i, x, y):
        return (x < y) if i == 2 else (x > y)

    def takes(i):
        return (a < chain - 1) if i == 2 else (a > 0)

    def step1(i, state):
        st_own[i] = state.astype(BF16)
        step1_copy(i).start()

    def step2(i):
        step1_copy(i).wait_recv()
        st_tot[i] = (st_own[i, my_half].astype(F32) + st_peer[i, my_half].astype(F32)).astype(BF16)
        for e in range(1, chain):
            for to in (a - e, a + e):

                @pl.when(after(i, to, a) & (to >= 0) & (to < chain))
                def _():
                    step2_copy(i, to, a).start()

    def step3(i):
        half32[...] = jnp.zeros_like(half32)
        for source in range(chain):

            @pl.when(after(i, a, source))
            def _():
                step2_copy(i, source, source).wait_recv()
                half32[...] += st_z[i, source].astype(F32)

        st_half[i] = half32[...].astype(BF16)

        @pl.when(takes(i))
        def _():
            step3_copy(i).start()

        @pl.when(jnp.logical_not(takes(i)))
        def _():
            st_far[i] = jnp.zeros_like(st_far[i])

    def step4(i):
        @pl.when(takes(i))
        def _():
            step3_copy(i).wait_recv()

        whole32[my_half] = st_half[i].astype(F32)
        whole32[far_half] = st_far[i].astype(F32)

        @pl.when(b == (0 if i == 2 else 1))
        def _():
            whole32[...] += st_peer[i].astype(F32)

        return whole32[...]

    def part(p, mb):
        return acc[p, pl.ds(mb * tokens, tokens)].astype(BF16)

    kb, vb = part(1, 1), part(2, 1)
    step1(0, t_dot(kb, vb))
    step1(1, t_dot(part(1, 0), part(2, 0)))

    def q_lap(d, carry):
        arrivals(d, q_only, ())
        crossings(d - 1, q_only)
        return carry

    lax.fori_loop(1, 2, q_lap, 0)
    step2(0)
    step2(1)
    lax.fori_loop(2, chain, q_lap, 0)
    step3(0)
    step3(1)
    crossings(chain - 1, q_only)

    for load in o_loads:
        load.wait()
    positions = lax.broadcasted_iota(jnp.int32, (tokens, tokens), 0)
    others = lax.broadcasted_iota(jnp.int32, (tokens, tokens), 1)
    causal = others <= positions

    def masked(scores):
        return jnp.where(causal, scores, 0.0).astype(BF16)

    gain = gain_ref[...]
    kb, vb, qb = part(1, 1), part(2, 1), part(0, 1)
    scores = masked(dot_t(qb, kb))
    prefix = (step4(0) + init[1, 0]).astype(BF16)
    output = dot(qb, prefix) + dot(scores, vb)
    scale = lax.rsqrt(jnp.mean(output * output, -1, keepdims=True) + epsilon)
    weighted = cot[...] * gain
    d_out = scale * weighted - output * (
        scale * scale * scale * jnp.mean(output * weighted, -1, keepdims=True)
    )
    d_out = d_out.astype(BF16)
    step1(2, t_dot(qb, d_out))
    d_scores = masked(dot_t(d_out, vb))
    dq = (dot_t(d_out, prefix) + dot(d_scores, kb)).astype(BF16)
    step2(2)
    dk_near = t_dot(d_scores, qb)
    dv_near = t_dot(scores, d_out)

    kf, vf, qf = part(1, 0), part(2, 0), part(0, 0)
    prefix_f = (step4(1) + init[0, 0]).astype(BF16)
    out_f = dot(qf, prefix_f) + dot(masked(dot_t(qf, kf)), vf)
    scale_f = lax.rsqrt(jnp.mean(out_f * out_f, -1, keepdims=True) + epsilon)
    of_ref[...] = out_f * scale_f * gain

    step3(2)
    suffix = step4(2).astype(BF16)
    dk = (dot_t(vb, suffix) + dk_near).astype(BF16)
    dv = (dot(kb, suffix) + dv_near).astype(BF16)

    def piece(j):
        rows = pl.ds(pl.multiple_of(j * feat, feat), feat)
        return dot_t(dq, wbuf[0, rows]) + dot_t(dk, wbuf[1, rows]) + dot_t(dv, wbuf[2, rows])

    def twin_copy(slot):
        return pltpu.make_async_remote_copy(
            src_ref=c_send.at[slot],
            dst_ref=c_recv.at[slot],
            send_sem=c_ssem.at[slot],
            recv_sem=c_rsem.at[slot],
            device_id=(s, twin),
            device_id_type=MESH,
        )

    def pair_copy(to, slot):
        return pltpu.make_async_remote_copy(
            src_ref=x_send.at[to],
            dst_ref=x_recv.at[slot],
            send_sem=x_ssem.at[to],
            recv_sem=x_rsem.at[slot],
            device_id=(s, to * 2 + c),
            device_id_type=MESH,
        )

    def twin_sum(to):
        c_send[to] = piece(to * 2 + 1 - c).astype(BF16)
        twin_copy(to).start()
        mine = piece(to * 2 + c)
        twin_copy(to).wait_recv()
        return mine + c_recv[to].astype(F32)

    def pair_lap(e, carry):
        to = lax.rem(xh + e, pairs)
        x_send[to] = twin_sum(to).astype(BF16)
        pair_copy(to, xh).start()
        return carry

    lax.fori_loop(1, pairs, pair_lap, 0)
    total = twin_sum(xh)
    for e in range(1, pairs):
        source = lax.rem(xh + e, pairs)
        pair_copy(source, source).wait_recv()
        total += x_recv[source].astype(F32)
    ob_ref[...] = total.astype(BF16)

    def drain_chain(sa, carry):
        for p in range(3):
            shard_copy(p, sa, b, CROSS).wait_send()

            @pl.when((sa <= a) & (a < chain - 1))
            def _():
                shard_copy(p, sa, b, UP).wait_send()

            @pl.when((sa >= a) & (a > 0))
            def _():
                shard_copy(p, sa, b, DOWN).wait_send()

        for i in range(3):

            @pl.when(after(i, sa, a))
            def _():
                step2_copy(i, sa, a).wait_send()

        return carry

    lax.fori_loop(0, chain, drain_chain, 0)
    for i in range(3):
        step1_copy(i).wait_send()

        @pl.when(takes(i))
        def _():
            step3_copy(i).wait_send()

    for slot in range(pairs):
        twin_copy(slot).wait_send()
    for e in range(1, pairs):
        pair_copy(lax.rem(xh + e, pairs), xh).wait_send()


def body(n, hn, fwd_tokens, bwd_tokens, qkv_weight, head_gain, out_cotangent, initial_state):
    tokens, model = fwd_tokens.shape
    width = head_gain.shape[0]
    feat = model // hn
    chain, pairs = n // 2, hn // 2
    anywhere = pl.BlockSpec(memory_space=pl.ANY)
    vmem = pl.BlockSpec(memory_space=pltpu.VMEM)
    dma = pltpu.SemaphoreType.DMA
    return pl.pallas_call(
        functools.partial(kernel, n, hn),
        out_shape=(
            jax.ShapeDtypeStruct((tokens, width), F32),
            jax.ShapeDtypeStruct((tokens, feat), BF16),
        ),
        in_specs=[anywhere, anywhere, anywhere, vmem, anywhere, anywhere],
        out_specs=(vmem, vmem),
        scratch_shapes=[
            pltpu.VMEM((2 * tokens, model), BF16),
            pltpu.VMEM((3, model, width), BF16),
            pltpu.VMEM((3, 2 * tokens, width), F32),
            pltpu.VMEM((tokens, width), F32),
            pltpu.VMEM((2, 1, width, width), F32),
            pltpu.VMEM((3, width, width), BF16),
            pltpu.VMEM((3, width, width), BF16),
            pltpu.VMEM((3, width // 2, width), BF16),
            pltpu.VMEM((3, chain, width // 2, width), BF16),
            pltpu.VMEM((3, width // 2, width), BF16),
            pltpu.VMEM((3, width // 2, width), BF16),
            pltpu.VMEM((width // 2, width), F32),
            pltpu.VMEM((width, width), F32),
            pltpu.VMEM((pairs, tokens, feat), BF16),
            pltpu.VMEM((pairs, tokens, feat), BF16),
            pltpu.VMEM((pairs, tokens, feat), BF16),
            pltpu.VMEM((pairs, tokens, feat), BF16),
            dma((7,)),
            dma((3, chain, 3)),
            dma((n, 3)),
            dma((3, 2)),
            dma((3, 2)),
            dma((3, chain)),
            dma((3, chain)),
            dma((pairs,)),
            dma((pairs,)),
            dma((pairs,)),
            dma((pairs,)),
        ],
        compiler_params=pltpu.CompilerParams(
            collective_id=0, has_side_effects=True, vmem_limit_bytes=48 * 1024 * 1024
        ),
    )(fwd_tokens, bwd_tokens, qkv_weight, head_gain.reshape(1, width), out_cotangent, initial_state)


def solution(mesh):
    return jax.shard_map(
        functools.partial(body, mesh.shape["seq"], mesh.shape["heads"]),
        mesh=mesh,
        in_specs=(
            P("seq", None),
            P("seq", None),
            P("seq", "heads"),
            P("heads"),
            P("seq", "heads"),
            P(None, "heads", None, None),
        ),
        out_specs=(P("seq", "heads"), P("seq", "heads")),
        check_vma=False,
    )
```

```python
import functools

import jax
import jax.numpy as jnp
from jax import lax
from jax.experimental import pallas as pl
from jax.experimental.pallas import tpu as pltpu
from jax.sharding import PartitionSpec as P

MESH = pl.DeviceIdType.MESH
BF16 = jnp.bfloat16
F32 = jnp.float32
epsilon = 1e-06


def dot(a, b):
    return lax.dot_general(a, b, (((1,), (0,)), ((), ())), preferred_element_type=F32)


def dot_t(a, b):
    return lax.dot_general(a, b, (((1,), (1,)), ((), ())), preferred_element_type=F32)


def t_dot(a, b):
    return lax.dot_general(a, b, (((0,), (0,)), ((), ())), preferred_element_type=F32)


def kernel(
    n,
    hn,
    xf_ref,
    xb_ref,
    w_ref,
    gain_ref,
    cot_ref,
    init_ref,
    of_ref,
    ob_ref,
    xbuf,
    wbuf,
    acc,
    cot,
    init,
    gain,
    st_own,
    st_peer,
    st_tot,
    st_z,
    st_half,
    st_far,
    half32,
    whole32,
    c_send,
    c_recv,
    x_send,
    x_recv,
    load_sem,
    wsend,
    wrecv,
    st_ssem,
    st_rsem,
    z_ssem,
    z_rsem,
    c_ssem,
    c_rsem,
    x_ssem,
    x_rsem,
):
    s, h = lax.axis_index("seq"), lax.axis_index("heads")
    chain, pairs = n // 2, hn // 2
    a, b = lax.div(s, 2), lax.rem(s, 2)
    xh, c = lax.div(h, 2), lax.rem(h, 2)
    mate = a * 2 + 1 - b
    twin = xh * 2 + 1 - c
    tokens = xf_ref.shape[0]
    depth = w_ref.shape[0]
    width = gain_ref.shape[1]
    half = width // 2
    feat = ob_ref.shape[1]

    def rows_of(source):
        return pl.ds(pl.multiple_of(source * depth, depth), depth)

    w_loads = [
        pltpu.make_async_copy(
            w_ref.at[:, pl.ds(p * width, width)], wbuf.at[p, rows_of(s)], load_sem.at[p]
        )
        for p in range(3)
    ]
    x_loads = [
        pltpu.make_async_copy(xf_ref, xbuf.at[pl.ds(0, tokens)], load_sem.at[3]),
        pltpu.make_async_copy(xb_ref, xbuf.at[pl.ds(tokens, tokens)], load_sem.at[4]),
    ]
    o_loads = [
        pltpu.make_async_copy(cot_ref, cot, load_sem.at[5]),
        pltpu.make_async_copy(init_ref, init, load_sem.at[6]),
        pltpu.make_async_copy(gain_ref, gain, load_sem.at[7]),
    ]
    for p in (1, 2, 0):
        w_loads[p].start()
    for load in x_loads + o_loads:
        load.start()

    barrier = pltpu.get_barrier_semaphore()

    def greet(seq_index, head_index):
        pl.semaphore_signal(barrier, inc=1, device_id=(seq_index, head_index), device_id_type=MESH)

    for e in range(1, chain):
        greet(lax.rem(a + e, chain) * 2 + b, h)
    greet(mate, h)
    for e in range(1, pairs):
        greet(s, lax.rem(xh + e, pairs) * 2 + c)
    greet(s, twin)
    pl.semaphore_wait(barrier, chain + pairs)

    UP, DOWN, CROSS = 0, 1, 2
    early = (2, 1)
    kv = ((1, 0), (1, 1), (2, 0), (2, 1))
    kv_crossing = ((1, 0), (1, 1), (2, 0))
    q_only = ((0, 0), (0, 1))
    sub = depth // 2

    def shard_copy(piece, sa, sb, way):
        p, r = piece
        source = sa * 2 + sb
        rows = pl.ds(pl.multiple_of(source * depth + r * sub, sub), sub)
        to = {UP: s + 2, DOWN: s - 2, CROSS: mate}[way]
        return pltpu.make_async_remote_copy(
            src_ref=wbuf.at[p, rows],
            dst_ref=wbuf.at[p, rows],
            send_sem=wsend.at[way, source, p, r],
            recv_sem=wrecv.at[source, p, r],
            device_id=(to, h),
            device_id_type=MESH,
        )

    def arrived(piece, sa, sb):
        shard_copy(piece, sa, sb, CROSS).wait_recv()

    def project(source, columns):
        x = xbuf[:, pl.ds(pl.multiple_of(source * depth, depth), depth)]
        for p in columns:
            acc[p] += dot(x, wbuf[p, rows_of(source)])

    def start_up(piece, sa, sb):
        @pl.when(a < chain - 1)
        def _():
            shard_copy(piece, sa, sb, UP).start()

    def start_down(piece, sa, sb):
        @pl.when(a > 0)
        def _():
            shard_copy(piece, sa, sb, DOWN).start()

    def pass_on(d, piece, sb, crosses):
        @pl.when(a - d >= 0)
        def _():
            arrived(piece, a - d, sb)
            start_up(piece, a - d, sb)
            if crosses:
                shard_copy(piece, a - d, sb, CROSS).start()

        @pl.when(a + d < chain)
        def _():
            arrived(piece, a + d, sb)
            start_down(piece, a + d, sb)
            if crosses:
                shard_copy(piece, a + d, sb, CROSS).start()

    def chain_products(d, columns):
        @pl.when(a - d >= 0)
        def _():
            project((a - d) * 2 + b, columns)

        @pl.when(a + d < chain)
        def _():
            project((a + d) * 2 + b, columns)

    def crossings(d, pieces, columns):
        def crossed(sa):
            for piece in pieces:
                arrived(piece, sa, 1 - b)
            project(sa * 2 + 1 - b, columns)

        @pl.when(a - d >= 0)
        def _():
            crossed(a - d)

        @pl.when((a + d < chain) & (d > 0))
        def _():
            crossed(a + d)

    for p in (1, 2):
        w_loads[p].wait()
        for r in range(2):
            start_up((p, r), a, b)
            start_down((p, r), a, b)
            shard_copy((p, r), a, b, CROSS).start()
    w_loads[0].wait()
    acc[...] = jnp.zeros_like(acc)
    for load in x_loads:
        load.wait()
    project(s, (1, 2))
    arrived(early, a, 1 - b)
    start_up(early, a, 1 - b)
    start_down(early, a, 1 - b)

    @pl.when(a == 0)
    def _():
        for piece in q_only:
            start_up(piece, a, b)

    @pl.when(a == chain - 1)
    def _():
        for piece in q_only:
            start_down(piece, a, b)

    def kv_lap(d, carry):
        for piece in kv:
            pass_on(d, piece, b, piece != early)
        pass_on(d, early, 1 - b, False)

        @pl.when(a - d == 0)
        def _():
            for piece in q_only:
                start_up(piece, a, b)

        @pl.when(a + d == chain - 1)
        def _():
            for piece in q_only:
                start_down(piece, a, b)

        chain_products(d, (1, 2))
        crossings(d - 1, kv_crossing, (1, 2))
        return carry

    lax.fori_loop(1, chain, kv_lap, 0)
    for piece in q_only:
        shard_copy(piece, a, b, CROSS).start()
    project(s, (0,))
    crossings(chain - 1, kv_crossing, (1, 2))

    my_half = pl.ds(pl.multiple_of(b * half, half), half)
    far_half = pl.ds(pl.multiple_of((1 - b) * half, half), half)

    def step1_copy(i):
        return pltpu.make_async_remote_copy(
            src_ref=st_own.at[i, far_half],
            dst_ref=st_peer.at[i],
            send_sem=st_ssem.at[i, 0],
            recv_sem=st_rsem.at[i, 0],
            device_id=(mate, h),
            device_id_type=MESH,
        )

    def step2_copy(i, to, slot):
        return pltpu.make_async_remote_copy(
            src_ref=st_tot.at[i],
            dst_ref=st_z.at[i, slot],
            send_sem=z_ssem.at[i, to],
            recv_sem=z_rsem.at[i, slot],
            device_id=(to * 2 + b, h),
            device_id_type=MESH,
        )

    def step3_copy(i):
        return pltpu.make_async_remote_copy(
            src_ref=st_half.at[i],
            dst_ref=st_far.at[i],
            send_sem=st_ssem.at[i, 1],
            recv_sem=st_rsem.at[i, 1],
            device_id=(mate, h),
            device_id_type=MESH,
        )

    def after(i, x, y):
        return (x < y) if i == 2 else (x > y)

    def later(i):
        return 0 if i == 2 else 1

    def step1(i, state):
        st_own[i] = state.astype(BF16)
        step1_copy(i).start()

    def step2(i):
        step1_copy(i).wait_recv()
        st_tot[i] = (st_own[i, my_half].astype(F32) + st_peer[i].astype(F32)).astype(BF16)
        for e in range(1, chain):
            for to in (a - e, a + e):

                @pl.when(after(i, to, a) & (to >= 0) & (to < chain))
                def _():
                    step2_copy(i, to, a).start()

    def step3(i):
        half32[...] = jnp.zeros_like(half32)
        for source in range(chain):

            @pl.when(after(i, a, source))
            def _():
                step2_copy(i, source, source).wait_recv()
                half32[...] += st_z[i, source].astype(F32)

        whole32[i, my_half] = half32[...]

        @pl.when(b == later(i))
        def _():
            st_half[i] = half32[...].astype(BF16)
            whole32[i, my_half] += st_peer[i].astype(F32)

        @pl.when(b != later(i))
        def _():
            st_half[i] = (half32[...] + st_own[i, my_half].astype(F32)).astype(BF16)

        step3_copy(i).start()

    def step4(i):
        step3_copy(i).wait_recv()
        whole32[i, far_half] = st_far[i].astype(F32)
        return whole32[i]

    def part(p, mb):
        return acc[p, pl.ds(mb * tokens, tokens)].astype(BF16)

    kb, vb = part(1, 1), part(2, 1)
    step1(0, t_dot(kb, vb))
    step1(1, t_dot(part(1, 0), part(2, 0)))

    def q_lap(d, carry):
        for piece in q_only:
            pass_on(d, piece, b, True)
        chain_products(d, (0,))
        crossings(d - 1, q_only, (0,))
        return carry

    lax.fori_loop(1, 2, q_lap, 0)
    step2(0)
    step2(1)
    lax.fori_loop(2, chain, q_lap, 0)
    step3(0)
    step3(1)
    crossings(chain - 1, q_only, (0,))

    for load in o_loads:
        load.wait()
    positions = lax.broadcasted_iota(jnp.int32, (tokens, tokens), 0)
    others = lax.broadcasted_iota(jnp.int32, (tokens, tokens), 1)
    causal = others <= positions

    def masked(scores):
        return jnp.where(causal, scores, 0.0).astype(BF16)

    gains = gain[...]
    kb, vb, qb = part(1, 1), part(2, 1), part(0, 1)
    scores = masked(dot_t(qb, kb))
    prefix = (step4(0) + init[1, 0]).astype(BF16)
    output = dot(qb, prefix) + dot(scores, vb)
    scale = lax.rsqrt(jnp.mean(output * output, -1, keepdims=True) + epsilon)
    weighted = cot[...] * gains
    d_out = scale * weighted - output * (
        scale * scale * scale * jnp.mean(output * weighted, -1, keepdims=True)
    )
    d_out = d_out.astype(BF16)
    step1(2, t_dot(qb, d_out))
    d_scores = masked(dot_t(d_out, vb))
    dq = (dot_t(d_out, prefix) + dot(d_scores, kb)).astype(BF16)
    step2(2)
    dk_near = t_dot(d_scores, qb)
    dv_near = t_dot(scores, d_out)

    kf, vf, qf = part(1, 0), part(2, 0), part(0, 0)
    prefix_f = (step4(1) + init[0, 0]).astype(BF16)
    out_f = dot(qf, prefix_f) + dot(masked(dot_t(qf, kf)), vf)
    scale_f = lax.rsqrt(jnp.mean(out_f * out_f, -1, keepdims=True) + epsilon)
    of_ref[...] = out_f * scale_f * gains

    step3(2)
    suffix = step4(2).astype(BF16)
    dk = (dot_t(vb, suffix) + dk_near).astype(BF16)
    dv = (dot(kb, suffix) + dv_near).astype(BF16)

    part_rows = tokens // 2
    grads = [[g[k * part_rows : (k + 1) * part_rows] for g in (dq, dk, dv)] for k in range(2)]

    def product(j, k):
        rows = pl.ds(pl.multiple_of(j * feat, feat), feat)
        return sum(dot_t(grads[k][p], wbuf[p, rows]) for p in range(3))

    def twin_copy(slot, k):
        return pltpu.make_async_remote_copy(
            src_ref=c_send.at[slot, k],
            dst_ref=c_recv.at[slot, k],
            send_sem=c_ssem.at[slot, k],
            recv_sem=c_rsem.at[slot, k],
            device_id=(s, twin),
            device_id_type=MESH,
        )

    def pair_copy(to, slot, k):
        return pltpu.make_async_remote_copy(
            src_ref=x_send.at[to, k],
            dst_ref=x_recv.at[slot, k],
            send_sem=x_ssem.at[to, k],
            recv_sem=x_rsem.at[slot, k],
            device_id=(s, to * 2 + c),
            device_id_type=MESH,
        )

    def for_twin(to):
        for k in range(2):
            c_send[to, k] = product(to * 2 + 1 - c, k).astype(BF16)
            twin_copy(to, k).start()

    def twin_sum(to, k):
        mine = product(to * 2 + c, k)
        twin_copy(to, k).wait_recv()
        return mine + c_recv[to, k].astype(F32)

    def pair_lap(e, carry):
        to = lax.rem(xh + e, pairs)
        for_twin(to)
        for k in range(2):
            x_send[to, k] = twin_sum(to, k).astype(BF16)
            pair_copy(to, xh, k).start()
        return carry

    lax.fori_loop(1, pairs, pair_lap, 0)
    for_twin(xh)
    totals = [twin_sum(xh, k) for k in range(2)]
    for k in range(2):
        total = totals[k]
        for e in range(1, pairs):
            source = lax.rem(xh + e, pairs)
            pair_copy(source, source, k).wait_recv()
            total += x_recv[source, k].astype(F32)
        ob_ref[pl.ds(k * part_rows, part_rows)] = total.astype(BF16)

    def drain_chain(sa, carry):
        def left_chain(piece, sb):
            @pl.when((sa <= a) & (a < chain - 1))
            def _():
                shard_copy(piece, sa, sb, UP).wait_send()

            @pl.when((sa >= a) & (a > 0))
            def _():
                shard_copy(piece, sa, sb, DOWN).wait_send()

        for piece in kv + q_only:
            left_chain(piece, b)
        left_chain(early, 1 - b)
        for piece in kv_crossing + q_only:
            shard_copy(piece, sa, b, CROSS).wait_send()
        for i in range(3):

            @pl.when(after(i, sa, a))
            def _():
                step2_copy(i, sa, a).wait_send()

        return carry

    lax.fori_loop(0, chain, drain_chain, 0)
    shard_copy(early, a, b, CROSS).wait_send()
    for i in range(3):
        step1_copy(i).wait_send()
        step3_copy(i).wait_send()
    for k in range(2):
        for slot in range(pairs):
            twin_copy(slot, k).wait_send()
        for e in range(1, pairs):
            pair_copy(lax.rem(xh + e, pairs), xh, k).wait_send()


def body(n, hn, fwd_tokens, bwd_tokens, qkv_weight, head_gain, out_cotangent, initial_state):
    tokens, model = fwd_tokens.shape
    width = head_gain.shape[0]
    feat = model // hn
    chain, pairs = n // 2, hn // 2
    hbm = pl.BlockSpec(memory_space=pltpu.HBM)
    vmem = pl.BlockSpec(memory_space=pltpu.VMEM)
    dma = pltpu.SemaphoreType.DMA
    return pl.pallas_call(
        functools.partial(kernel, n, hn),
        out_shape=(
            jax.ShapeDtypeStruct((tokens, width), F32),
            jax.ShapeDtypeStruct((tokens, feat), BF16),
        ),
        in_specs=[hbm] * 6,
        out_specs=(vmem, vmem),
        scratch_shapes=[
            pltpu.VMEM((2 * tokens, model), BF16),
            pltpu.VMEM((3, model, width), BF16),
            pltpu.VMEM((3, 2 * tokens, width), F32),
            pltpu.VMEM((tokens, width), F32),
            pltpu.VMEM((2, 1, width, width), F32),
            pltpu.VMEM((1, width), F32),
            pltpu.VMEM((3, width, width), BF16),
            pltpu.VMEM((3, width // 2, width), BF16),
            pltpu.VMEM((3, width // 2, width), BF16),
            pltpu.VMEM((3, chain, width // 2, width), BF16),
            pltpu.VMEM((3, width // 2, width), BF16),
            pltpu.VMEM((3, width // 2, width), BF16),
            pltpu.VMEM((width // 2, width), F32),
            pltpu.VMEM((3, width, width), F32),
            pltpu.VMEM((pairs, 2, tokens // 2, feat), BF16),
            pltpu.VMEM((pairs, 2, tokens // 2, feat), BF16),
            pltpu.VMEM((pairs, 2, tokens // 2, feat), BF16),
            pltpu.VMEM((pairs, 2, tokens // 2, feat), BF16),
            dma((8,)),
            dma((3, n, 3, 2)),
            dma((n, 3, 2)),
            dma((3, 2)),
            dma((3, 2)),
            dma((3, chain)),
            dma((3, chain)),
            dma((pairs, 2)),
            dma((pairs, 2)),
            dma((pairs, 2)),
            dma((pairs, 2)),
        ],
        compiler_params=pltpu.CompilerParams(
            collective_id=0, has_side_effects=True, vmem_limit_bytes=63 * 1024 * 1024 + 512 * 1024
        ),
    )(fwd_tokens, bwd_tokens, qkv_weight, head_gain.reshape(1, width), out_cotangent, initial_state)


def solution(mesh):
    return jax.shard_map(
        functools.partial(body, mesh.shape["seq"], mesh.shape["heads"]),
        mesh=mesh,
        in_specs=(
            P("seq", None),
            P("seq", None),
            P("seq", "heads"),
            P("heads"),
            P("seq", "heads"),
            P(None, "heads", None, None),
        ),
        out_specs=(P("seq", "heads"), P("seq", "heads")),
        check_vma=False,
    )
```

```python
import functools

import jax
import jax.numpy as jnp
from jax import lax
from jax.experimental import pallas as pl
from jax.experimental.pallas import tpu as pltpu
from jax.sharding import PartitionSpec as P

MESH = pl.DeviceIdType.MESH
BF16 = jnp.bfloat16
F32 = jnp.float32
epsilon = 1e-06


def dot(a, b):
    return lax.dot_general(a, b, (((1,), (0,)), ((), ())), preferred_element_type=F32)


def dot_t(a, b):
    return lax.dot_general(a, b, (((1,), (1,)), ((), ())), preferred_element_type=F32)


def t_dot(a, b):
    return lax.dot_general(a, b, (((0,), (0,)), ((), ())), preferred_element_type=F32)


def kernel(
    n,
    hn,
    xf_ref,
    xb_ref,
    w_ref,
    gain_ref,
    cot_ref,
    init_ref,
    of_ref,
    ob_ref,
    xbuf,
    wbuf,
    acc,
    cot,
    init,
    gain,
    st_own,
    st_peer,
    st_tot,
    st_z,
    st_half,
    st_far,
    half32,
    whole32,
    c_send,
    c_recv,
    x_send,
    x_recv,
    load_sem,
    wsend,
    wrecv,
    st_ssem,
    st_rsem,
    z_ssem,
    z_rsem,
    c_ssem,
    c_rsem,
    x_ssem,
    x_rsem,
):
    s, h = lax.axis_index("seq"), lax.axis_index("heads")
    chain, pairs = n // 2, hn // 2
    a, b = lax.div(s, 2), lax.rem(s, 2)
    xh, c = lax.div(h, 2), lax.rem(h, 2)
    mate = a * 2 + 1 - b
    twin = xh * 2 + 1 - c
    tokens = xf_ref.shape[0]
    depth = w_ref.shape[0]
    width = gain_ref.shape[1]
    half = width // 2
    feat = ob_ref.shape[1]

    def rows_of(source):
        return pl.ds(pl.multiple_of(source * depth, depth), depth)

    w_loads = [
        pltpu.make_async_copy(
            w_ref.at[:, pl.ds(p * width, width)], wbuf.at[p, rows_of(s)], load_sem.at[p]
        )
        for p in range(3)
    ]
    x_loads = [
        pltpu.make_async_copy(xf_ref, xbuf.at[pl.ds(0, tokens)], load_sem.at[3]),
        pltpu.make_async_copy(xb_ref, xbuf.at[pl.ds(tokens, tokens)], load_sem.at[4]),
    ]
    o_loads = [
        pltpu.make_async_copy(cot_ref, cot, load_sem.at[5]),
        pltpu.make_async_copy(init_ref, init, load_sem.at[6]),
        pltpu.make_async_copy(gain_ref, gain, load_sem.at[7]),
    ]
    for p in (1, 2, 0):
        w_loads[p].start()
    for load in x_loads + o_loads:
        load.start()

    barrier = pltpu.get_barrier_semaphore()

    def greet(seq_index, head_index):
        pl.semaphore_signal(barrier, inc=1, device_id=(seq_index, head_index), device_id_type=MESH)

    for e in range(1, chain):
        greet(lax.rem(a + e, chain) * 2 + b, h)
    greet(mate, h)
    for e in range(1, pairs):
        greet(s, lax.rem(xh + e, pairs) * 2 + c)
    greet(s, twin)
    pl.semaphore_wait(barrier, chain + pairs)

    UP, DOWN, CROSS = 0, 1, 2
    early = (2, 1)
    kv = ((1, 0), (1, 1), (2, 0), (2, 1))
    kv_crossing = ((1, 0), (1, 1), (2, 0))
    q_only = ((0, 0), (0, 1))
    sub = depth // 2

    def shard_copy(piece, sa, sb, way):
        p, r = piece
        source = sa * 2 + sb
        rows = pl.ds(pl.multiple_of(source * depth + r * sub, sub), sub)
        to = {UP: s + 2, DOWN: s - 2, CROSS: mate}[way]
        return pltpu.make_async_remote_copy(
            src_ref=wbuf.at[p, rows],
            dst_ref=wbuf.at[p, rows],
            send_sem=wsend.at[way, source, p, r],
            recv_sem=wrecv.at[source, p, r],
            device_id=(to, h),
            device_id_type=MESH,
        )

    def arrived(piece, sa, sb):
        shard_copy(piece, sa, sb, CROSS).wait_recv()

    def project(source, columns):
        x = xbuf[:, pl.ds(pl.multiple_of(source * depth, depth), depth)]
        for p in columns:
            acc[p] += dot(x, wbuf[p, rows_of(source)])

    def start_up(piece, sa, sb):
        @pl.when(a < chain - 1)
        def _():
            shard_copy(piece, sa, sb, UP).start()

    def start_down(piece, sa, sb):
        @pl.when(a > 0)
        def _():
            shard_copy(piece, sa, sb, DOWN).start()

    def pass_on(d, piece, sb, crosses):
        @pl.when(a - d >= 0)
        def _():
            arrived(piece, a - d, sb)
            start_up(piece, a - d, sb)
            if crosses:
                shard_copy(piece, a - d, sb, CROSS).start()

        @pl.when(a + d < chain)
        def _():
            arrived(piece, a + d, sb)
            start_down(piece, a + d, sb)
            if crosses:
                shard_copy(piece, a + d, sb, CROSS).start()

    def chain_products(d, columns):
        @pl.when(a - d >= 0)
        def _():
            project((a - d) * 2 + b, columns)

        @pl.when(a + d < chain)
        def _():
            project((a + d) * 2 + b, columns)

    def crossings(d, pieces, columns):
        def crossed(sa):
            for piece in pieces:
                arrived(piece, sa, 1 - b)
            project(sa * 2 + 1 - b, columns)

        @pl.when(a - d >= 0)
        def _():
            crossed(a - d)

        @pl.when((a + d < chain) & (d > 0))
        def _():
            crossed(a + d)

    for p in (1, 2):
        w_loads[p].wait()
        for r in range(2):
            start_up((p, r), a, b)
            start_down((p, r), a, b)
            shard_copy((p, r), a, b, CROSS).start()
    w_loads[0].wait()
    acc[...] = jnp.zeros_like(acc)
    for load in x_loads:
        load.wait()
    project(s, (1, 2))
    arrived(early, a, 1 - b)
    start_up(early, a, 1 - b)
    start_down(early, a, 1 - b)

    @pl.when(a == 0)
    def _():
        for piece in q_only:
            start_up(piece, a, b)

    @pl.when(a == chain - 1)
    def _():
        for piece in q_only:
            start_down(piece, a, b)

    def kv_lap(d, carry):
        for piece in kv:
            pass_on(d, piece, b, piece != early)
        pass_on(d, early, 1 - b, False)

        @pl.when(a - d == 0)
        def _():
            for piece in q_only:
                start_up(piece, a, b)

        @pl.when(a + d == chain - 1)
        def _():
            for piece in q_only:
                start_down(piece, a, b)

        @pl.when(d == 1)
        def _():
            for piece in q_only:
                shard_copy(piece, a, b, CROSS).start()

        chain_products(d, (1, 2))
        crossings(d - 1, kv_crossing, (1, 2))
        return carry

    lax.fori_loop(1, chain, kv_lap, 0)
    project(s, (0,))
    crossings(chain - 1, kv_crossing, (1, 2))

    my_half = pl.ds(pl.multiple_of(b * half, half), half)
    far_half = pl.ds(pl.multiple_of((1 - b) * half, half), half)

    def step1_copy(i):
        return pltpu.make_async_remote_copy(
            src_ref=st_own.at[i, far_half],
            dst_ref=st_peer.at[i],
            send_sem=st_ssem.at[i, 0],
            recv_sem=st_rsem.at[i, 0],
            device_id=(mate, h),
            device_id_type=MESH,
        )

    def step2_copy(i, to, slot):
        return pltpu.make_async_remote_copy(
            src_ref=st_tot.at[i],
            dst_ref=st_z.at[i, slot],
            send_sem=z_ssem.at[i, to],
            recv_sem=z_rsem.at[i, slot],
            device_id=(to * 2 + b, h),
            device_id_type=MESH,
        )

    def step3_copy(i):
        return pltpu.make_async_remote_copy(
            src_ref=st_half.at[i],
            dst_ref=st_far.at[i],
            send_sem=st_ssem.at[i, 1],
            recv_sem=st_rsem.at[i, 1],
            device_id=(mate, h),
            device_id_type=MESH,
        )

    def after(i, x, y):
        return (x < y) if i == 2 else (x > y)

    def later(i):
        return 0 if i == 2 else 1

    def step1(i, state):
        st_own[i] = state.astype(BF16)
        step1_copy(i).start()

    def step2(i):
        step1_copy(i).wait_recv()
        st_tot[i] = (st_own[i, my_half].astype(F32) + st_peer[i].astype(F32)).astype(BF16)
        for e in range(1, chain):
            for to in (a - e, a + e):

                @pl.when(after(i, to, a) & (to >= 0) & (to < chain))
                def _():
                    step2_copy(i, to, a).start()

    def step3(i):
        half32[...] = jnp.zeros_like(half32)
        for source in range(chain):

            @pl.when(after(i, a, source))
            def _():
                step2_copy(i, source, source).wait_recv()
                half32[...] += st_z[i, source].astype(F32)

        whole32[i, my_half] = half32[...]

        @pl.when(b == later(i))
        def _():
            st_half[i] = half32[...].astype(BF16)
            whole32[i, my_half] += st_peer[i].astype(F32)

        @pl.when(b != later(i))
        def _():
            st_half[i] = (half32[...] + st_own[i, my_half].astype(F32)).astype(BF16)

        step3_copy(i).start()

    def step4(i):
        step3_copy(i).wait_recv()
        whole32[i, far_half] = st_far[i].astype(F32)
        return whole32[i]

    def part(p, mb):
        return acc[p, pl.ds(mb * tokens, tokens)].astype(BF16)

    kb, vb = part(1, 1), part(2, 1)
    step1(0, t_dot(kb, vb))

    def q_lap(d, carry):
        for piece in q_only:
            pass_on(d, piece, b, True)
        chain_products(d, (0,))
        crossings(d - 1, q_only, (0,))
        return carry

    lax.fori_loop(1, 2, q_lap, 0)
    step2(0)
    lax.fori_loop(2, chain, q_lap, 0)
    step3(0)
    crossings(chain - 1, q_only, (0,))

    for load in o_loads:
        load.wait()
    positions = lax.broadcasted_iota(jnp.int32, (tokens, tokens), 0)
    others = lax.broadcasted_iota(jnp.int32, (tokens, tokens), 1)
    causal = others <= positions

    def masked(scores):
        return jnp.where(causal, scores, 0.0).astype(BF16)

    gains = gain[...]
    kb, vb, qb = part(1, 1), part(2, 1), part(0, 1)
    scores = masked(dot_t(qb, kb))
    prefix = (step4(0) + init[1, 0]).astype(BF16)
    output = dot(qb, prefix) + dot(scores, vb)
    scale = lax.rsqrt(jnp.mean(output * output, -1, keepdims=True) + epsilon)
    weighted = cot[...] * gains
    d_out = scale * weighted - output * (
        scale * scale * scale * jnp.mean(output * weighted, -1, keepdims=True)
    )
    d_out = d_out.astype(BF16)
    step1(2, t_dot(qb, d_out))
    d_scores = masked(dot_t(d_out, vb))
    dq = (dot_t(d_out, prefix) + dot(d_scores, kb)).astype(BF16)
    step2(2)
    dk_near = t_dot(d_scores, qb)
    dv_near = t_dot(scores, d_out)

    step1(1, t_dot(part(1, 0), part(2, 0)))
    step3(2)
    suffix = step4(2).astype(BF16)
    dk = (dot_t(vb, suffix) + dk_near).astype(BF16)
    dv = (dot(kb, suffix) + dv_near).astype(BF16)
    step2(1)

    part_rows = tokens // 2
    grads = [[g[k * part_rows : (k + 1) * part_rows] for g in (dq, dk, dv)] for k in range(2)]

    def product(j, k):
        rows = pl.ds(pl.multiple_of(j * feat, feat), feat)
        return sum(dot_t(grads[k][p], wbuf[p, rows]) for p in range(3))

    def twin_copy(slot, k):
        return pltpu.make_async_remote_copy(
            src_ref=c_send.at[slot, k],
            dst_ref=c_recv.at[slot, k],
            send_sem=c_ssem.at[slot, k],
            recv_sem=c_rsem.at[slot, k],
            device_id=(s, twin),
            device_id_type=MESH,
        )

    def pair_copy(to, slot, k):
        return pltpu.make_async_remote_copy(
            src_ref=x_send.at[to, k],
            dst_ref=x_recv.at[slot, k],
            send_sem=x_ssem.at[to, k],
            recv_sem=x_rsem.at[slot, k],
            device_id=(s, to * 2 + c),
            device_id_type=MESH,
        )

    def for_twin(to):
        for k in range(2):
            c_send[to, k] = product(to * 2 + 1 - c, k).astype(BF16)
            twin_copy(to, k).start()

    def twin_sum(to, k):
        mine = product(to * 2 + c, k)
        twin_copy(to, k).wait_recv()
        return mine + c_recv[to, k].astype(F32)

    def pair_lap(e, carry):
        to = lax.rem(xh + e, pairs)
        for_twin(to)
        for k in range(2):
            x_send[to, k] = twin_sum(to, k).astype(BF16)
            pair_copy(to, xh, k).start()
        return carry

    lax.fori_loop(1, pairs, pair_lap, 0)
    for_twin(xh)
    totals = [twin_sum(xh, k) for k in range(2)]
    step3(1)
    kf, vf, qf = part(1, 0), part(2, 0), part(0, 0)
    prefix_f = (step4(1) + init[0, 0]).astype(BF16)
    out_f = dot(qf, prefix_f) + dot(masked(dot_t(qf, kf)), vf)
    scale_f = lax.rsqrt(jnp.mean(out_f * out_f, -1, keepdims=True) + epsilon)
    of_ref[...] = out_f * scale_f * gains

    for k in range(2):
        total = totals[k]
        for e in range(1, pairs):
            source = lax.rem(xh + e, pairs)
            pair_copy(source, source, k).wait_recv()
            total += x_recv[source, k].astype(F32)
        ob_ref[pl.ds(k * part_rows, part_rows)] = total.astype(BF16)

    def drain_chain(sa, carry):
        def left_chain(piece, sb):
            @pl.when((sa <= a) & (a < chain - 1))
            def _():
                shard_copy(piece, sa, sb, UP).wait_send()

            @pl.when((sa >= a) & (a > 0))
            def _():
                shard_copy(piece, sa, sb, DOWN).wait_send()

        for piece in kv + q_only:
            left_chain(piece, b)
        left_chain(early, 1 - b)
        for piece in kv_crossing + q_only:
            shard_copy(piece, sa, b, CROSS).wait_send()
        for i in range(3):

            @pl.when(after(i, sa, a))
            def _():
                step2_copy(i, sa, a).wait_send()

        return carry

    lax.fori_loop(0, chain, drain_chain, 0)
    shard_copy(early, a, b, CROSS).wait_send()
    for i in range(3):
        step1_copy(i).wait_send()
        step3_copy(i).wait_send()
    for k in range(2):
        for slot in range(pairs):
            twin_copy(slot, k).wait_send()
        for e in range(1, pairs):
            pair_copy(lax.rem(xh + e, pairs), xh, k).wait_send()


def body(n, hn, fwd_tokens, bwd_tokens, qkv_weight, head_gain, out_cotangent, initial_state):
    tokens, model = fwd_tokens.shape
    width = head_gain.shape[0]
    feat = model // hn
    chain, pairs = n // 2, hn // 2
    hbm = pl.BlockSpec(memory_space=pltpu.HBM)
    vmem = pl.BlockSpec(memory_space=pltpu.VMEM)
    dma = pltpu.SemaphoreType.DMA
    return pl.pallas_call(
        functools.partial(kernel, n, hn),
        out_shape=(
            jax.ShapeDtypeStruct((tokens, width), F32),
            jax.ShapeDtypeStruct((tokens, feat), BF16),
        ),
        in_specs=[hbm] * 6,
        out_specs=(vmem, vmem),
        scratch_shapes=[
            pltpu.VMEM((2 * tokens, model), BF16),
            pltpu.VMEM((3, model, width), BF16),
            pltpu.VMEM((3, 2 * tokens, width), F32),
            pltpu.VMEM((tokens, width), F32),
            pltpu.VMEM((2, 1, width, width), F32),
            pltpu.VMEM((1, width), F32),
            pltpu.VMEM((3, width, width), BF16),
            pltpu.VMEM((3, width // 2, width), BF16),
            pltpu.VMEM((3, width // 2, width), BF16),
            pltpu.VMEM((3, chain, width // 2, width), BF16),
            pltpu.VMEM((3, width // 2, width), BF16),
            pltpu.VMEM((3, width // 2, width), BF16),
            pltpu.VMEM((width // 2, width), F32),
            pltpu.VMEM((3, width, width), F32),
            pltpu.VMEM((pairs, 2, tokens // 2, feat), BF16),
            pltpu.VMEM((pairs, 2, tokens // 2, feat), BF16),
            pltpu.VMEM((pairs, 2, tokens // 2, feat), BF16),
            pltpu.VMEM((pairs, 2, tokens // 2, feat), BF16),
            dma((8,)),
            dma((3, n, 3, 2)),
            dma((n, 3, 2)),
            dma((3, 2)),
            dma((3, 2)),
            dma((3, chain)),
            dma((3, chain)),
            dma((pairs, 2)),
            dma((pairs, 2)),
            dma((pairs, 2)),
            dma((pairs, 2)),
        ],
        compiler_params=pltpu.CompilerParams(
            collective_id=0, has_side_effects=True, vmem_limit_bytes=63 * 1024 * 1024 + 512 * 1024
        ),
    )(fwd_tokens, bwd_tokens, qkv_weight, head_gain.reshape(1, width), out_cotangent, initial_state)


def solution(mesh):
    return jax.shard_map(
        functools.partial(body, mesh.shape["seq"], mesh.shape["heads"]),
        mesh=mesh,
        in_specs=(
            P("seq", None),
            P("seq", None),
            P("seq", "heads"),
            P("heads"),
            P("seq", "heads"),
            P(None, "heads", None, None),
        ),
        out_specs=(P("seq", "heads"), P("seq", "heads")),
        check_vma=False,
    )
```
